128 devices in a mesh: aln: 2 (over core), row: 32 (over z, x, y_lo), head: 2 (over y_hi).
Axes of the slice: x: 4, y: 4 (y_hi: 2, y_lo: 2; y = y_hi * 2 + y_lo), z: 4, core: 2. Of those that a mesh axis runs over, the one named last changes fastest.
Arguments:
- tokens: bfloat16 [2, 192, 512, 768], P('aln', 'row'), may hold values from -7 to 7
- w_query: bfloat16 [768, 768], P(None, 'head'), may hold values from -0.25259074 to 0.25259074
- w_key: bfloat16 [768, 768], P(None, 'head'), may hold values from -0.25259074 to 0.25259074
- w_value: bfloat16 [768, 768], P(None, 'head'), may hold values from -0.21875 to 0.21875
- w_out: bfloat16 [768, 768], P('head'), may hold values from -0.21875 to 0.21875
- cotangent: bfloat16 [2, 192, 512, 768], P('aln', 'row'), may hold values from -12 to 12
Outputs:
- token_grads: bfloat16 [2, 192, 512, 768], P('aln', 'row', None, 'head')
- weight_grads: float32 [768, 4, 768], P(('aln', 'row'), None, 'head')
The draws below stay inside these ranges and needn't reach their ends.
All inputs are finite; a program needn't handle non-finite values.
Results may differ from the reference program's by a relative error of at most 0.014.
Values may be sent and summed in bfloat16 or wider, within the bound.
A program may use at most 128 MiB of HBM per device.

```python
import math
import jax
import jax.numpy as jnp
from jax import lax

D = 768
HEADS = 12
HDIM = 64
COLS = 512
ROWS = 192
ALIGNS = 2


def shared_query(key):
    return jnp.clip(jax.random.normal(key, (D, D), jnp.float32), -5.0, 5.0) / math.sqrt(D)


def draw_w_query(key, part):
    base_matrix = shared_query(key)
    return base_matrix.astype(jnp.bfloat16)


def draw_w_key(key, part):
    key = jax.random.fold_in(key, 12)
    other_matrix = jnp.clip(jax.random.normal(key, (D, D), jnp.float32), -5.0, 5.0) / math.sqrt(D)
    blended = other_matrix
    return blended.astype(jnp.bfloat16)


def draw_tokens(key, part):
    key = jax.random.fold_in(key, 13)
    noise_key = jax.random.fold_in(key, 0)
    array_shape = (ALIGNS, ROWS, COLS, D)
    values = jnp.clip(jax.random.normal(noise_key, array_shape, jnp.float32), -6.0, 6.0)
    return values.astype(jnp.bfloat16)


def raised(array, own_key, source, target, parts, factor):
    def block_of(axis_at):
        return (jnp.arange(array.shape[axis_at]) // (array.shape[axis_at] // parts)).reshape((-1,) + (1,) * (array.ndim - 1 - axis_at))

    one_side = jax.random.permutation(own_key, parts)[block_of(target)]
    other_side = (block_of(target) + parts // 2) % parts
    return jnp.where((block_of(source) == one_side) | (block_of(source) == other_side), factor * array, array)


def shard_levels(key, extent, cuts, smallest, largest):
    def one(position, parts):
        heights = jax.random.uniform(jax.random.fold_in(jax.random.fold_in(key, 6), position), (parts,), jnp.float32, smallest / len(cuts), largest / len(cuts))
        return jnp.repeat(jnp.exp(heights), extent[position] // parts).reshape((-1,) + (1,) * (len(extent) - position - 1))

    factor_of = one(*cuts[0])
    for cut in cuts[1:]:
        factor_of = factor_of * one(*cut)
    return factor_of


def noise(key, shape, scale, most, cuts=(), held_as=jnp.bfloat16):
    array = jax.random.normal(key, shape, jnp.float32) * scale
    if len(cuts) > 0:
        array = shard_levels(key, shape, cuts, -0.22, 0.18) * array
    return jnp.clip(array, min=-most, max=most).astype(held_as)


def heavy_noise(key, shape, deviation, bound, cuts, heavy, kind=jnp.bfloat16):
    result = deviation * jax.random.normal(key, shape, jnp.float32)
    if cuts:
        result = result * shard_levels(key, shape, cuts, -0.22, 0.18)
    return jnp.clip(raised(result, jax.random.fold_in(key, 3), *heavy), -bound, bound).astype(kind)


def setup_inputs(seed: int = 0) -> dict:
    keys = jax.random.split(jax.random.key(seed), 7)
    tokens = draw_tokens(jax.random.fold_in(keys[6], 71), 0)
    w_query = draw_w_query(jax.random.fold_in(keys[6], 71), 0)
    w_key = draw_w_key(jax.random.fold_in(keys[6], 71), 0)
    w_value = noise(keys[3], (D, D), D ** -0.5, 0.21875, ((1, 2),))
    w_out = noise(keys[4], (D, D), D ** -0.5, 0.21875, ((0, 2),))
    cotangent = heavy_noise(keys[5], (ALIGNS, ROWS, COLS, D), 2.0, 12.0, ((0, 2), (1, 32)), (1, 3, 32, 2.75))
    return dict(tokens=tokens, w_query=w_query, w_key=w_key, w_value=w_value, w_out=w_out, cotangent=cotangent)


def softmax_rows(scores):
    highest = lax.optimization_barrier(jnp.max(scores, axis=-1, keepdims=True))
    powers = jnp.exp(scores - highest)
    return powers / lax.optimization_barrier(jnp.sum(powers, axis=-1, keepdims=True))

def rounded(values):
    return lax.optimization_barrier(values.astype(jnp.bfloat16))

def reference(tokens, w_query, w_key, w_value, w_out, cotangent):
    scaling = 1.0 / math.sqrt(HDIM * ROWS)

    def one_alignment(inputs_pair):
        alignment, upstream = inputs_pair
        flat_tokens = alignment.reshape(ROWS * COLS, D)
        flat_upstream = upstream.reshape(ROWS * COLS, D)

        def project(weight):
            product = jnp.dot(flat_tokens, weight, preferred_element_type=jnp.float32)
            return rounded(product).reshape(ROWS, COLS, HEADS, HDIM)
        queries = project(w_query)
        key_rows = project(w_key)
        value_rows = project(w_value)
        scores = jnp.einsum('rihc,rjhc->hij', queries.astype(jnp.float32), key_rows.astype(jnp.float32)) * scaling
        attention = rounded(softmax_rows(scores))
        outgrad = rounded(jnp.dot(flat_upstream, w_out.T, preferred_element_type=jnp.float32)).reshape(ROWS, COLS, HEADS, HDIM)
        mixed_rows = rounded(jnp.einsum('hij,rjhc->rihc', attention.astype(jnp.float32), value_rows.astype(jnp.float32)))
        prob_grads = jnp.einsum('rihc,rjhc->hij', outgrad.astype(jnp.float32), value_rows.astype(jnp.float32))
        weights_full = attention.astype(jnp.float32)
        centre = lax.optimization_barrier(jnp.sum(weights_full * prob_grads, axis=-1, keepdims=True))
        slopes = rounded(weights_full * (prob_grads - centre) * scaling)
        query_grad = rounded(jnp.einsum('hij,rjhc->rihc', slopes.astype(jnp.float32), key_rows.astype(jnp.float32))).reshape(ROWS * COLS, D)
        key_grad = rounded(jnp.einsum('hij,rihc->rjhc', slopes.astype(jnp.float32), queries.astype(jnp.float32))).reshape(ROWS * COLS, D)
        value_grad = rounded(jnp.einsum('hij,rihc->rjhc', weights_full, outgrad.astype(jnp.float32))).reshape(ROWS * COLS, D)
        input_total = jnp.dot(query_grad, w_query.T, preferred_element_type=jnp.float32)
        input_total = input_total + jnp.dot(key_grad, w_key.T, preferred_element_type=jnp.float32)
        input_total = input_total + jnp.dot(value_grad, w_value.T, preferred_element_type=jnp.float32)
        token_grad = input_total.astype(jnp.bfloat16).reshape(ROWS, COLS, D)
        tokens_wide = flat_tokens.astype(jnp.float32)
        grad_query = jnp.einsum('tk,tn->kn', tokens_wide, query_grad.astype(jnp.float32))
        grad_key = jnp.einsum('tk,tn->kn', tokens_wide, key_grad.astype(jnp.float32))
        grad_value = jnp.einsum('tk,tn->kn', tokens_wide, value_grad.astype(jnp.float32))
        grad_output = jnp.einsum('tk,tn->kn', flat_upstream.astype(jnp.float32), mixed_rows.reshape(ROWS * COLS, D).astype(jnp.float32))
        stacked = jnp.stack([grad_query, grad_key, grad_value, grad_output], axis=1)
        return (token_grad, stacked)
    token_grads, per_alignment = lax.map(one_alignment, (tokens, cotangent))
    return (token_grads, lax.optimization_barrier(jnp.sum(per_alignment, axis=0)))
```

```python
import functools
import math

import jax
import jax.numpy as jnp
from jax import lax
from jax.experimental import pallas as pl
from jax.experimental.pallas import tpu as pltpu
from jax.sharding import PartitionSpec as P

HDIM = 64
MESH = pl.DeviceIdType.MESH
F32 = jnp.float32
BF16 = jnp.bfloat16

ROWS = 6
COLS = 512
D = 768
LOCAL = 384
PAIRS = 3
PAIR = 128
WIDE = ROWS * PAIR

NT = (((1,), (1,)), ((), ()))
TN = (((0,), (0,)), ((), ()))


def position():
    row = lax.axis_index("row")
    return row // 8, (row // 2) % 4, row % 2


def neighbours():
    z, x, low = position()

    def at(z, x, low):
        return (lax.axis_index("aln"), z * 8 + x * 2 + low, lax.axis_index("head"))

    z_axis = (z, at((z + 1) % 4, x, low), at((z + 3) % 4, x, low))
    x_axis = (x, at(z, (x + 1) % 4, low), at(z, (x + 3) % 4, low))
    return z_axis, x_axis, (low, at(z, x, 1 - low))


def remote(src, dst, send, recv, index, device):
    return pltpu.make_async_remote_copy(
        src_ref=src,
        dst_ref=dst,
        send_sem=send.at[index],
        recv_sem=recv.at[index],
        device_id=device,
        device_id_type=MESH,
    )


def greet(devices):
    barrier = pltpu.get_barrier_semaphore()
    for device in devices:
        pl.semaphore_signal(barrier, inc=1, device_id=device, device_id_type=MESH)
    pl.semaphore_wait(barrier, len(devices))


class Sum:
    def __init__(self, part, got, send, recv, base, first, second, pair):
        self.part, self.got = part, got
        self.send, self.recv, self.base = send, recv, base
        self.c1, self.p1, self.m1 = first
        self.c2, self.p2, self.m2 = second
        self.low, self.partner = pair
        self.pending = []
        self.sent = []

    def go(self, source, landing, size, slot, device):
        copy = remote(
            self.part(source, size), self.got(landing, size), self.send, self.recv,
            self.base + (slot,), device,
        )
        copy.start()
        self.pending.append(copy)
        self.sent.append(copy)

    def arrive(self):
        for copy in self.pending:
            copy.wait_recv()
        self.pending = []

    def add(self, at, size, *landings):
        total = self.part(at, size)[...].astype(F32)
        for landing in landings:
            total = total + self.got(landing, size)[...].astype(F32)
        return total

    def put(self, at, size, *landings):
        self.part(at, size)[...] = self.add(at, size, *landings).astype(BF16)

    def step1(self):
        far = ((self.c1 + 2) % 4) * 128
        self.go(far, 0, 64, 0, self.p1)
        self.go(far + 64, 64, 64, 1, self.m1)

    def step2(self):
        self.arrive()
        up, down = ((self.c1 + 1) % 4) * 128, ((self.c1 + 3) % 4) * 128
        self.put(up, 64, 0)
        self.go(up, 128, 128, 2, self.p1)
        self.put(down + 64, 64, 64)
        self.go(down, 256, 128, 3, self.m1)

    def step3(self):
        self.arrive()
        self.put(self.c1 * 128, 128, 128, 256)
        far = self.c1 * 128 + ((self.c2 + 2) % 4) * 32
        self.go(far, 384, 16, 4, self.p2)
        self.go(far + 16, 400, 16, 5, self.m2)

    def step4(self):
        self.arrive()
        up = self.c1 * 128 + ((self.c2 + 1) % 4) * 32
        down = self.c1 * 128 + ((self.c2 + 3) % 4) * 32
        self.put(up, 16, 384)
        self.go(up, 416, 32, 6, self.p2)
        self.put(down + 16, 16, 400)
        self.go(down, 448, 32, 7, self.m2)

    def step5(self):
        self.arrive()
        here = self.c1 * 128 + self.c2 * 32
        self.put(here, 32, 416, 448)
        self.go(here + (1 - self.low) * 16, 480, 16, 8, self.partner)

    def own(self):
        return self.c1 * 128 + self.c2 * 32 + self.low * 16

    def finish(self):
        self.arrive()
        return self.add(self.own(), 16, 480)


class Gather:
    def __init__(self, part, send, recv, base, first, second, pair):
        self.part = part
        self.send, self.recv, self.base = send, recv, base
        self.c1, self.p1, self.m1 = first
        self.c2, self.p2, self.m2 = second
        self.low, self.partner = pair
        self.pending = []
        self.sent = []

    def go(self, at, size, slot, device):
        copy = remote(
            self.part(at, size), self.part(at, size), self.send, self.recv,
            self.base + (slot,), device,
        )
        copy.start()
        self.pending.append(copy)
        self.sent.append(copy)

    def arrive(self):
        for copy in self.pending:
            copy.wait_recv()
        self.pending = []

    def step1(self):
        self.go(self.c1 * 128 + self.c2 * 32 + self.low * 16, 16, 9, self.partner)

    def step2(self):
        self.arrive()
        here = self.c1 * 128 + self.c2 * 32
        self.go(here, 32, 10, self.p2)
        self.go(here, 32, 11, self.m2)

    def step3(self):
        self.arrive()
        self.go(self.c1 * 128 + ((self.c2 + 3) % 4) * 32, 16, 12, self.p2)
        self.go(self.c1 * 128 + ((self.c2 + 1) % 4) * 32 + 16, 16, 13, self.m2)

    def step4(self):
        self.arrive()
        self.go(self.c1 * 128, 128, 14, self.p1)
        self.go(self.c1 * 128, 128, 15, self.m1)

    def step5(self):
        self.arrive()
        self.go(((self.c1 + 3) % 4) * 128, 64, 16, self.p1)
        self.go(((self.c1 + 1) % 4) * 128 + 64, 64, 17, self.m1)

    def step6(self):
        self.arrive()


def rows_of(ref, lead, columns=None):
    def view(start, size):
        rows = pl.ds(pl.multiple_of(start, 16) if not isinstance(start, int) else start, size)
        if columns is None:
            return ref.at[lead, rows, :]
        return ref.at[lead, rows, columns]

    return view


def attention_kernel(
    scaling,
    tokens, cotangent, w_query, w_key, w_value, w_out,
    grads,
    tok, cot, wqk, wv, wo, queries, keys, values, outgrads,
    parts, landed, maps, staged,
    send, recv, load, store,
):
    z_axis, x_axis, pair = neighbours()

    loads = []

    def fetch(src, dst):
        copy = pltpu.make_async_copy(src, dst, load.at[len(loads)])
        copy.start()
        loads.append(copy)
        return copy

    need = {0: [], 1: [], 2: [], 3: [], 4: [], 5: []}
    for p in range(PAIRS):
        lanes = pl.ds(p * PAIR, PAIR)
        need[2 * p].append(fetch(w_query.at[:, lanes], wqk.at[p, :, pl.ds(0, PAIR)]))
        need[2 * p].append(fetch(w_key.at[:, lanes], wqk.at[p, :, pl.ds(PAIR, PAIR)]))
        if p == 0:
            need[0].append(fetch(tokens, tok))
            need[1].append(fetch(cotangent, cot))
            need[1].append(fetch(w_value, wv))
            need[1].append(fetch(w_out, wo))

    greet([z_axis[1], z_axis[2], x_axis[1], x_axis[2], pair[1]])

    lane = lax.broadcasted_iota(jnp.int32, (1, WIDE), 1)
    even = (lane % PAIR) < HDIM
    masks = [even.astype(F32).astype(BF16), (1.0 - even.astype(F32)).astype(BF16)]

    sums, gathers = {}, {}
    for u in range(2 * PAIRS):
        for hh in range(2):
            g = 2 * u + hh
            axes = (z_axis, x_axis) if hh == 0 else (x_axis, z_axis)
            sums[u, hh] = Sum(
                rows_of(parts, g), rows_of(landed, g), send, recv, (g,), *axes, pair
            )
            gathers[u, hh] = Gather(rows_of(maps, g), send, recv, (g,), *axes, pair)

    def compute(u):
        p = u // 2
        for copy in need[u]:
            copy.wait()
        if u % 2 == 0:
            def project(r, carry):
                out = jnp.dot(
                    tok[pl.ds(pl.multiple_of(r * COLS, COLS), COLS), :], wqk[p],
                    preferred_element_type=F32,
                ).astype(BF16)
                lanes = pl.ds(pl.multiple_of(r * PAIR, PAIR), PAIR)
                queries[p, :, lanes] = out[:, :PAIR]
                keys[p, :, lanes] = out[:, PAIR:]
                return carry

            left, right = queries, keys
        else:
            def project(r, carry):
                rows = pl.ds(pl.multiple_of(r * COLS, COLS), COLS)
                lanes = pl.ds(pl.multiple_of(r * PAIR, PAIR), PAIR)
                values[p, :, lanes] = jnp.dot(
                    tok[rows, :], wv[:, p * PAIR:(p + 1) * PAIR], preferred_element_type=F32
                ).astype(BF16)
                outgrads[p, :, lanes] = lax.dot_general(
                    cot[rows, :], wo[p * PAIR:(p + 1) * PAIR, :], NT, preferred_element_type=F32
                ).astype(BF16)
                return carry

            left, right = outgrads, values
        lax.fori_loop(0, ROWS, project, 0)
        for hh in range(2):
            masked = right[p] * masks[hh]

            def product(b, carry):
                rows = pl.ds(pl.multiple_of(b * 256, 256), 256)
                parts[2 * u + hh, rows, :] = lax.dot_general(
                    left[p, rows, :], masked, NT, preferred_element_type=F32
                ).astype(BF16)
                return carry

            for b in range(2):
                product(b, 0)
            sums[u, hh].step1()

    def finish(u):
        for hh in range(2):
            total = sums[u, hh].finish()
            rows = pl.ds(pl.multiple_of(sums[u, hh].own(), 16), 16)
            if u % 2 == 0:
                scores = total * scaling
                powers = jnp.exp(scores - jnp.max(scores, axis=-1, keepdims=True))
                result = powers / jnp.sum(powers, axis=-1, keepdims=True)
            else:
                attention = maps[2 * (u - 1) + hh, rows, :].astype(F32)
                centre = jnp.sum(attention * total, axis=-1, keepdims=True)
                result = attention * (total - centre) * scaling
            maps[2 * u + hh, rows, :] = result.astype(BF16)
            gathers[u, hh].step1()

    stores = []

    def emit(k, p, b, rows, value):
        value = value.astype(BF16)
        for r in range(ROWS):
            staged[k, p, r, rows, :] = value[:, r * PAIR:(r + 1) * PAIR]

    def apply(u):
        p = u // 2
        if u % 2 == 0:
            forward, backward, k_forward, k_backward = values, outgrads, 3, 2
        else:
            forward, backward, k_forward, k_backward = keys, queries, 0, 1
        ahead = [forward[p] * masks[hh] for hh in range(2)]
        for b in range(2):
            rows = pl.ds(b * 256, 256)
            out = jnp.dot(maps[2 * u, rows, :], ahead[0], preferred_element_type=F32)
            out = out + jnp.dot(maps[2 * u + 1, rows, :], ahead[1], preferred_element_type=F32)
            emit(k_forward, p, b, rows, out)
        back = [backward[p] * masks[hh] for hh in range(2)]
        for b in range(2):
            rows = pl.ds(b * 256, 256)
            out = lax.dot_general(maps[2 * u, :, rows], back[0], TN, preferred_element_type=F32)
            out = out + lax.dot_general(
                maps[2 * u + 1, :, rows], back[1], TN, preferred_element_type=F32
            )
            emit(k_backward, p, b, rows, out)
        for k in (k_forward, k_backward):
            copy = pltpu.make_async_copy(
                staged.at[k, p],
                grads.at[:, :, pl.ds(k * LOCAL + p * PAIR, PAIR)],
                store.at[k, p],
            )
            copy.start()
            stores.append(copy)

    stages = (
        [lambda u, n=n: [getattr(sums[u, hh], n)() for hh in range(2)]
         for n in ("step2", "step3", "step4", "step5")]
        + [finish]
        + [lambda u, n=n: [getattr(gathers[u, hh], n)() for hh in range(2)]
           for n in ("step2", "step3", "step4", "step5", "step6")]
    )
    units = 2 * PAIRS
    compute(0)
    compute(1)
    for tick in range(units + len(stages) - 1):
        done = None
        for u in range(units):
            s = tick - u
            if 0 <= s < len(stages):
                stages[s](u)
                if s == len(stages) - 1:
                    done = u
        if tick + 2 < units:
            compute(tick + 2)
        if done is not None:
            apply(done)

    for item in list(sums.values()) + list(gathers.values()):
        for copy in item.sent:
            copy.wait_send()
    for copy in stores:
        copy.wait()


def output_kernel(
    tokens, cotangent, w_query, w_key, w_value, grads,
    token_out, weight_out,
    tok, cot, weights, both, leaving, arrived, result,
    core_leaving, core_arrived, mine, parts, landed, final,
    send, recv, load, store, token_send, token_recv, core_send, core_recv,
):
    z_axis, x_axis, pair = neighbours()
    aln, row, head = lax.axis_index("aln"), lax.axis_index("row"), lax.axis_index("head")
    head_partner = (aln, row, 1 - head)
    core_partner = (1 - aln, row, head)

    copies = []

    def fetch(src, dst):
        copy = pltpu.make_async_copy(src, dst, load.at[len(copies)])
        copy.start()
        copies.append(copy)
        return copy

    weight_loads = [
        fetch(w, weights.at[:, pl.ds(k * LOCAL, LOCAL)])
        for k, w in enumerate((w_query, w_key, w_value))
    ]
    grad_loads = [fetch(grads.at[r], both.at[r]) for r in range(ROWS)]
    token_load = fetch(tokens, tok)
    cotangent_load = fetch(cotangent, cot)

    greet([z_axis[1], z_axis[2], x_axis[1], x_axis[2], pair[1], head_partner, core_partner])

    for copy in weight_loads:
        copy.wait()
    three = 3 * LOCAL
    token_copies = []
    other = pl.ds(pl.multiple_of((1 - head) * LOCAL, LOCAL), LOCAL)
    ours = pl.ds(pl.multiple_of(head * LOCAL, LOCAL), LOCAL)
    for r in range(ROWS):
        grad_loads[r].wait()
        leaving[r] = lax.dot_general(
            both[r, :, :three], weights[other, :], NT, preferred_element_type=F32
        ).astype(BF16)
        copy = remote(
            leaving.at[r], arrived.at[r], token_send, token_recv, (r,), head_partner
        )
        copy.start()
        token_copies.append(copy)

    token_load.wait()
    cotangent_load.wait()
    flat = both[...].reshape(ROWS * COLS, 4 * LOCAL)

    def weight_grads(half):
        lanes = pl.ds(pl.multiple_of(half * LOCAL, LOCAL), LOCAL)
        inner = lax.dot_general(
            tok[:, lanes], flat[:, :three], TN, preferred_element_type=F32
        )
        outer = lax.dot_general(
            cot[:, lanes], flat[:, three:], TN, preferred_element_type=F32
        )
        return inner, outer

    inner, outer = weight_grads(1 - aln)
    core_leaving[:, :three] = inner.astype(BF16)
    core_leaving[:, three:] = outer.astype(BF16)
    core_copy = remote(
        core_leaving, core_arrived, core_send, core_recv, (0,), core_partner
    )
    core_copy.start()
    inner, outer = weight_grads(aln)
    mine[pl.ds(0, LOCAL), pl.ds(0, three)] = inner
    mine[pl.ds(0, LOCAL), pl.ds(three, LOCAL)] = outer
    mine[pl.ds(LOCAL, 8), :] = jnp.zeros((8, 4 * LOCAL), F32)
    core_copy.wait_recv()
    mine[pl.ds(0, LOCAL), :] += core_arrived[...].astype(F32)

    for z in range(4):
        for x in range(4):
            for low in range(2):
                block = mine[pl.ds((z * 8 + x * 2 + low) * 12, 16), :].astype(BF16)
                parts[0, pl.ds((z * 8 + x * 2 + low) * 16, 16), :] = block[:, :2 * LOCAL]
                parts[1, pl.ds((x * 8 + z * 2 + low) * 16, 16), :] = block[:, 2 * LOCAL:]
    sums = [
        Sum(rows_of(parts, g), rows_of(landed, g), send, recv, (g,), *axes, pair)
        for g, axes in enumerate(((z_axis, x_axis), (x_axis, z_axis)))
    ]

    outs = []

    def own_part(r):
        result[r] = lax.dot_general(
            both[r, :, :three], weights[ours, :], NT, preferred_element_type=F32
        )

    def own_finish(r):
        token_copies[r].wait_recv()
        leaving_free = arrived[r].astype(F32) + result[r]
        final[r] = leaving_free.astype(BF16)
        copy = pltpu.make_async_copy(final.at[r], token_out.at[r], store.at[r])
        copy.start()
        outs.append(copy)

    for step, name in enumerate(("step1", "step2", "step3", "step4", "step5")):
        for item in sums:
            getattr(item, name)()
        own_part(step)
    own_part(5)
    for g, item in enumerate(sums):
        weight_out[:, g * 2 * LOCAL:(g + 1) * 2 * LOCAL] = item.finish()
    for r in range(ROWS):
        own_finish(r)

    for copy in token_copies + [core_copy] + sums[0].sent + sums[1].sent:
        copy.wait_send()
    for copy in outs:
        copy.wait()


def local(tokens, w_query, w_key, w_value, w_out, cotangent):
    leading, rows_here, columns, model_width = tokens.shape
    scaling = 1.0 / math.sqrt(HDIM * rows_here * lax.axis_size("row"))
    flat_tokens = tokens.reshape(-1, model_width)
    flat_cotangent = cotangent.reshape(-1, model_width)
    anywhere = pl.BlockSpec(memory_space=pl.ANY)
    dma = pltpu.SemaphoreType.DMA

    grads = pl.pallas_call(
        functools.partial(attention_kernel, scaling),
        out_shape=jax.ShapeDtypeStruct((ROWS, COLS, 4 * LOCAL), BF16),
        in_specs=[anywhere] * 6,
        out_specs=anywhere,
        scratch_shapes=[
            pltpu.VMEM((ROWS * COLS, D), BF16),
            pltpu.VMEM((ROWS * COLS, D), BF16),
            pltpu.VMEM((PAIRS, D, 2 * PAIR), BF16),
            pltpu.VMEM((D, LOCAL), BF16),
            pltpu.VMEM((LOCAL, D), BF16),
            pltpu.VMEM((PAIRS, COLS, WIDE), BF16),
            pltpu.VMEM((PAIRS, COLS, WIDE), BF16),
            pltpu.VMEM((PAIRS, COLS, WIDE), BF16),
            pltpu.VMEM((PAIRS, COLS, WIDE), BF16),
            pltpu.VMEM((4 * PAIRS, COLS, COLS), BF16),
            pltpu.VMEM((4 * PAIRS, 496, COLS), BF16),
            pltpu.VMEM((4 * PAIRS, COLS, COLS), BF16),
            pltpu.VMEM((4, PAIRS, ROWS, COLS, PAIR), BF16),
            dma((4 * PAIRS, 18)),
            dma((4 * PAIRS, 18)),
            dma((10,)),
            dma((4, PAIRS)),
        ],
        compiler_params=pltpu.CompilerParams(
            collective_id=0, has_side_effects=True, vmem_limit_bytes=60 * 2**20
        ),
        cost_estimate=pl.CostEstimate(
            flops=14 * 10**9, bytes_accessed=22 * 10**6, transcendentals=10**6
        ),
        name="attention_maps",
    )(flat_tokens, flat_cotangent, w_query, w_key, w_value, w_out)

    token_grads, weight_grads = pl.pallas_call(
        output_kernel,
        out_shape=(
            jax.ShapeDtypeStruct((ROWS, COLS, LOCAL), BF16),
            jax.ShapeDtypeStruct((16, 4 * LOCAL), F32),
        ),
        in_specs=[anywhere] * 6,
        out_specs=(anywhere, pl.BlockSpec(memory_space=pltpu.VMEM)),
        scratch_shapes=[
            pltpu.VMEM((ROWS * COLS, D), BF16),
            pltpu.VMEM((ROWS * COLS, D), BF16),
            pltpu.VMEM((D, 3 * LOCAL), BF16),
            pltpu.VMEM((ROWS, COLS, 4 * LOCAL), BF16),
            pltpu.VMEM((ROWS, COLS, LOCAL), BF16),
            pltpu.VMEM((ROWS, COLS, LOCAL), BF16),
            pltpu.VMEM((ROWS, COLS, LOCAL), F32),
            pltpu.VMEM((LOCAL, 4 * LOCAL), BF16),
            pltpu.VMEM((LOCAL, 4 * LOCAL), BF16),
            pltpu.VMEM((LOCAL + 8, 4 * LOCAL), F32),
            pltpu.VMEM((2, COLS, 2 * LOCAL), BF16),
            pltpu.VMEM((2, 496, 2 * LOCAL), BF16),
            pltpu.VMEM((ROWS, COLS, LOCAL), BF16),
            dma((2, 9)),
            dma((2, 9)),
            dma((11,)),
            dma((ROWS,)),
            dma((ROWS,)),
            dma((ROWS,)),
            dma((1,)),
            dma((1,)),
        ],
        compiler_params=pltpu.CompilerParams(
            collective_id=1, has_side_effects=True, vmem_limit_bytes=60 * 2**20
        ),
        cost_estimate=pl.CostEstimate(
            flops=13 * 10**9, bytes_accessed=24 * 10**6, transcendentals=0
        ),
        name="output_grads",
    )(flat_tokens, flat_cotangent, w_query, w_key, w_value, grads)

    out_rows = model_width // lax.axis_size(("aln", "row"))
    token_grads = token_grads.reshape(leading, rows_here, columns, LOCAL)
    return token_grads, weight_grads[:out_rows].reshape(out_rows, 4, LOCAL)


def solution(mesh):
    return jax.shard_map(
        local,
        mesh=mesh,
        in_specs=(
            P("aln", "row", None, None),
            P(None, "head"),
            P(None, "head"),
            P(None, "head"),
            P("head", None),
            P("aln", "row", None, None),
        ),
        out_specs=(P("aln", "row", None, "head"), P(("aln", "row"), None, "head")),
        check_vma=False,
    )
```

```python
import functools
import math

import jax
import jax.numpy as jnp
from jax import lax
from jax.experimental import pallas as pl
from jax.experimental.pallas import tpu as pltpu
from jax.sharding import PartitionSpec as P

HDIM = 64
MESH = pl.DeviceIdType.MESH
F32 = jnp.float32
BF16 = jnp.bfloat16

ROWS = 6
COLS = 512
D = 768
LOCAL = 384
PAIRS = 3
PAIR = 128
WIDE = ROWS * PAIR

NT = (((1,), (1,)), ((), ()))
TN = (((0,), (0,)), ((), ()))

SCHEDULE = (
    ("stage", 0, 0), ("compute", 2), ("stage", 0, 1), ("compute", 3),
    ("stage", 1, 0), ("compute", 4), ("stage", 0, 2), ("stage", 1, 1), ("compute", 5),
    ("stage", 2, 0), ("stage", 0, 3), ("stage", 1, 2),
    ("stage", 2, 1), ("stage", 0, 4), ("stage", 1, 3),
    ("stage", 0, 5), ("stage", 1, 4), ("stage", 0, 6),
    ("stage", 2, 2), ("stage", 1, 5), ("stage", 0, 7),
    ("stage", 2, 3), ("stage", 1, 6), ("stage", 0, 8),
    ("stage", 2, 4), ("stage", 1, 7), ("apply", 0),
    ("stage", 2, 5), ("apply", 1),
    ("stage", 2, 6), ("stage", 1, 8), ("apply", 2),
    ("stage", 2, 7), ("apply", 3),
    ("stage", 2, 8), ("apply", 4), ("apply", 5),
)


def position():
    row = lax.axis_index("row")
    return row // 8, (row // 2) % 4, row % 2


class Way:
    def __init__(self, place, ring, across, others, low, partner):
        self.place, (self.after, self.before) = place, ring
        self.across, self.others = across, others
        self.low, self.partner = low, partner


def neighbours():
    z, x, low = position()

    def at(z, x, low):
        return (lax.axis_index("aln"), z * 8 + x * 2 + low, lax.axis_index("head"))

    far = (2, 1, 3)
    z_ring = [at((z + d) % 4, x, low) for d in far]
    x_ring = [at(z, (x + d) % 4, low) for d in far]
    partner = at(z, x, 1 - low)
    z_others = [((z + d) % 4, device) for d, device in zip(far, z_ring)]
    x_others = [((x + d) % 4, device) for d, device in zip(far, x_ring)]
    return (
        Way(z, z_ring[1:], x, x_others, low, partner),
        Way(x, x_ring[1:], z, z_others, low, partner),
    )


def remote(src, dst, send, recv, index, device):
    return pltpu.make_async_remote_copy(
        src_ref=src,
        dst_ref=dst,
        send_sem=send.at[index],
        recv_sem=recv.at[index],
        device_id=device,
        device_id_type=MESH,
    )


class Transfers:
    def __init__(self, send, recv, base, way):
        self.send, self.recv, self.base, self.way = send, recv, base, way
        self.pending = []
        self.sent = []

    def go(self, source, landing, slot, device):
        copy = remote(source, landing, self.send, self.recv, self.base + (slot,), device)
        copy.start()
        self.pending.append(copy)
        self.sent.append(copy)

    def arrive(self):
        for copy in self.pending:
            copy.wait_recv()
        self.pending = []

    def block(self, step):
        return ((self.way.place + step) % 4) * 128

    def half(self, low):
        return self.block(0) + low * 64

    def own(self):
        return self.half(self.way.low) + self.way.across * 16


class Sum(Transfers):
    def __init__(self, part, got, *rest, late=False):
        super().__init__(*rest)
        self.part, self.got, self.late = part, got, late

    def add(self, at, size, *landings):
        total = self.part(at, size)[...].astype(F32)
        for landing in landings:
            total = total + self.got(landing, size)[...].astype(F32)
        return total

    def put(self, at, size, *landings):
        self.part(at, size)[...] = self.add(at, size, *landings).astype(BF16)

    def step1(self):
        far = self.block(2)
        self.go(self.part(far, 64), self.got(0, 64), 0, self.way.after)
        self.go(self.part(far + 64, 64), self.got(64, 64), 1, self.way.before)

    def step2(self):
        self.arrive()
        self.put(self.block(1), 64, 0)
        self.go(self.part(self.block(1), 128), self.got(128, 128), 2, self.way.after)
        self.put(self.block(3) + 64, 64, 64)
        self.go(self.part(self.block(3), 128), self.got(256, 128), 3, self.way.before)

    def step3(self):
        self.arrive()
        self.put(self.block(0), 128, 128, 256)
        low = self.way.low
        if self.late:
            for j, (place, device) in enumerate(self.way.others):
                for k, which in enumerate((low, 1 - low)):
                    self.go(
                        self.part(self.half(which) + place * 16, 16),
                        self.got(384 + 48 * k + 16 * j, 16), 4 + 3 * k + j, device,
                    )
        else:
            self.go(self.part(self.half(1 - low), 64), self.got(384, 64), 4, self.way.partner)

    def step4(self):
        self.arrive()
        low = self.way.low
        if self.late:
            there = self.half(1 - low) + self.way.across * 16
            self.put(there, 16, 432, 448, 464)
            self.go(self.part(there, 16), self.got(480, 16), 10, self.way.partner)
            return
        self.put(self.half(low), 64, 384)
        for j, (place, device) in enumerate(self.way.others):
            self.go(
                self.part(self.half(low) + place * 16, 16), self.got(448 + 16 * j, 16),
                5 + j, device,
            )

    def finish(self):
        self.arrive()
        landings = (384, 400, 416, 480) if self.late else (448, 464, 480)
        return self.add(self.own(), 16, *landings)


class Gather(Transfers):
    def __init__(self, part, *rest):
        super().__init__(*rest)
        self.part = part

    def same(self, at, size, slot, device):
        self.go(self.part(at, size), self.part(at, size), slot, device)

    def step1(self):
        for j, (_, device) in enumerate(self.way.others):
            self.same(self.own(), 16, 8 + j, device)

    def step2(self):
        self.arrive()
        self.same(self.half(self.way.low), 64, 11, self.way.partner)

    def step3(self):
        self.arrive()
        self.same(self.block(0), 128, 12, self.way.after)
        self.same(self.block(0), 128, 13, self.way.before)

    def step4(self):
        self.arrive()
        self.same(self.block(3), 64, 14, self.way.after)
        self.same(self.block(1) + 64, 64, 15, self.way.before)

    def step5(self):
        self.arrive()


def rows_of(ref, *lead):
    def view(start, size):
        at = start if isinstance(start, int) else pl.multiple_of(start, 16)
        return ref.at[(*lead, pl.ds(at, size), slice(None))]

    return view


def backward_kernel(
    scaling,
    tokens, cotangent, w_query, w_key, w_value, w_out,
    token_out, weight_out,
    tok, cot, weights, wo, queries, keys, values, outgrads,
    parts, landed, maps, both, arrived, core_arrived, weight_landed, mine, last_own,
    send, recv, load, token_send, token_recv, core_send, core_recv,
    weight_send, weight_recv, store,
):
    ways = neighbours()
    aln, row, head = lax.axis_index("aln"), lax.axis_index("row"), lax.axis_index("head")
    head_partner = (aln, row, 1 - head)
    core_partner = (1 - aln, row, head)

    loads = []

    def fetch(src, dst):
        copy = pltpu.make_async_copy(src, dst, load.at[len(loads)])
        copy.start()
        loads.append(copy)
        return copy

    need = {u: [] for u in range(2 * PAIRS)}
    for p in range(PAIRS):
        lanes = pl.ds(p * PAIR, PAIR)
        need[2 * p].append(
            fetch(w_query.at[:, lanes], weights.at[:, pl.ds(2 * p * PAIR, PAIR)])
        )
        need[2 * p].append(
            fetch(w_key.at[:, lanes], weights.at[:, pl.ds((2 * p + 1) * PAIR, PAIR)])
        )
        if p == 0:
            token_loads = [
                fetch(tokens.at[pl.ds(r * COLS, COLS), :], tok.at[pl.ds(r * COLS, COLS), :])
                for r in range(ROWS)
            ]
            need[1].append(fetch(cotangent, cot))
            need[1].append(fetch(w_value, weights.at[:, pl.ds(2 * LOCAL, LOCAL)]))
            need[1].append(fetch(w_out, wo))

    barrier = pltpu.get_barrier_semaphore()
    others = [device for way in ways for _, device in way.others]
    others += [ways[0].partner, head_partner, core_partner]
    for device in others:
        pl.semaphore_signal(barrier, inc=1, device_id=device, device_id_type=MESH)

    lane = lax.broadcasted_iota(jnp.int32, (1, WIDE), 1)
    even = ((lane % PAIR) < HDIM).astype(F32)
    masks = [even.astype(BF16), (1.0 - even).astype(BF16)]

    sums, gathers = {}, {}
    for p in range(PAIRS):
        for hh in range(2):
            lead = (hh, p, slice(None))
            sums[p, hh] = Sum(
                rows_of(parts, *lead), rows_of(landed, *lead), send, recv, (hh, p), ways[hh]
            )
            gathers[p, hh] = Gather(rows_of(maps, *lead), send, recv, (hh, p), ways[hh])

    def project(p, size, first):
        rows = pl.ds(first * COLS, 3 * COLS)
        if size is None:
            out = jnp.dot(
                tok[rows, :], weights[:, 2 * p * PAIR:2 * (p + 1) * PAIR],
                preferred_element_type=F32,
            ).astype(BF16)
            targets = ((queries, p, out[:, :PAIR]), (keys, p, out[:, PAIR:]))
        else:
            value = jnp.dot(
                tok[rows, :],
                weights[:, 2 * LOCAL + p * PAIR:2 * LOCAL + (p + size) * PAIR],
                preferred_element_type=F32,
            ).astype(BF16)
            outgrad = lax.dot_general(
                cot[rows, :], wo[p * PAIR:(p + size) * PAIR, :], NT,
                preferred_element_type=F32,
            ).astype(BF16)
            targets = []
            for q in range(size):
                lanes = slice(q * PAIR, (q + 1) * PAIR)
                targets += [(values, p + q, value[:, lanes]), (outgrads, p + q, outgrad[:, lanes])]
        for ref, at, out in targets:
            for r in range(3):
                lanes = slice((first + r) * PAIR, (first + r + 1) * PAIR)
                ref[at, :, lanes] = out[r * COLS:(r + 1) * COLS, :]

    def compute(u):
        p, kind = u // 2, u % 2
        for copy in need[u]:
            copy.wait()
        size = None if kind == 0 else {0: 2, 1: 0, 2: 1}[p]
        if size != 0:
            for first in (0, 3):
                if u == 0:
                    for r in range(3):
                        token_loads[first + r].wait()
                project(p, size, first)
        left, right = (queries, keys) if kind == 0 else (outgrads, values)
        for hh in range(2):
            masked = right[p] * masks[hh]
            for b in range(2):
                rows = pl.ds(b * 256, 256)
                parts[hh, p, kind, rows, :] = lax.dot_general(
                    left[p, rows, :], masked, NT, preferred_element_type=F32
                ).astype(BF16)

    def finish(p):
        for hh in range(2):
            total = sums[p, hh].finish()
            rows = pl.ds(pl.multiple_of(sums[p, hh].own(), 16), 16)
            scores = total[0] * scaling
            powers = jnp.exp(scores - jnp.max(scores, axis=-1, keepdims=True))
            attention = (powers / jnp.sum(powers, axis=-1, keepdims=True)).astype(BF16)
            maps[hh, p, 0, rows, :] = attention
            attention = attention.astype(F32)
            centre = jnp.sum(attention * total[1], axis=-1, keepdims=True)
            maps[hh, p, 1, rows, :] = (attention * (total[1] - centre) * scaling).astype(BF16)
            gathers[p, hh].step1()

    def emit(lane_at, b, value):
        value = value.astype(BF16)
        for r in range(ROWS):
            both[r * COLS + b * 256:r * COLS + (b + 1) * 256, lane_at:lane_at + PAIR] = (
                value[:, r * PAIR:(r + 1) * PAIR]
            )

    def apply(u):
        p, kind = u // 2, u % 2
        if kind == 0:
            forward, backward = values, outgrads
            lane_forward, lane_backward = 3 * LOCAL + p * PAIR, 2 * LOCAL + p * PAIR
        else:
            forward, backward = keys, queries
            lane_forward, lane_backward = 2 * p * PAIR, (2 * p + 1) * PAIR
        ahead = [forward[p] * masks[hh] for hh in range(2)]
        for b in range(2):
            rows = pl.ds(b * 256, 256)
            out = jnp.dot(maps[0, p, kind, rows, :], ahead[0], preferred_element_type=F32)
            out = out + jnp.dot(maps[1, p, kind, rows, :], ahead[1], preferred_element_type=F32)
            emit(lane_forward, b, out)
        back = [backward[p] * masks[hh] for hh in range(2)]
        for b in range(2):
            rows = pl.ds(b * 256, 256)
            out = lax.dot_general(maps[0, p, kind, :, rows], back[0], TN, preferred_element_type=F32)
            out = out + lax.dot_general(
                maps[1, p, kind, :, rows], back[1], TN, preferred_element_type=F32
            )
            emit(lane_backward, b, out)

    other_lanes = pl.ds(pl.multiple_of((1 - aln) * LOCAL, LOCAL), LOCAL)
    own_lanes = pl.ds(pl.multiple_of(aln * LOCAL, LOCAL), LOCAL)

    def weight_part(part, lane_at, size, source, column):
        right = pl.ds(column, size)
        queries[part, pl.ds(0, LOCAL), pl.ds(lane_at, size)] = lax.dot_general(
            source[:, other_lanes], both[:, right], TN, preferred_element_type=F32
        ).astype(BF16)
        mine[part, pl.ds(0, LOCAL), pl.ds(lane_at, size)] = lax.dot_general(
            source[:, own_lanes], both[:, right], TN, preferred_element_type=F32
        )

    core_copies = {}

    def core_start(part):
        core_copies[part] = remote(
            queries.at[part, pl.ds(0, LOCAL), :], core_arrived.at[part],
            core_send, core_recv, (part,), core_partner,
        )
        core_copies[part].start()

    weight_sums = [
        Sum(
            rows_of(keys, part), rows_of(weight_landed, part), weight_send, weight_recv,
            (part,), way, late=True,
        )
        for part, way in enumerate(ways)
    ]

    def core_finish(part):
        core_copies[part].wait_recv()
        mine[part, pl.ds(0, LOCAL), :] += core_arrived[part].astype(F32)
        mine[part, pl.ds(LOCAL, 8), :] = jnp.zeros((8, 2 * LOCAL), F32)
        for z in range(4):
            for x in range(4):
                for low in range(2):
                    at = (z * 128 + x * 16, x * 128 + z * 16)[part] + low * 64
                    keys[part, at:at + 16, :] = mine[
                        part, pl.ds((z * 8 + x * 2 + low) * 12, 16), :
                    ].astype(BF16)

    def stage(p, number):
        if number == 4:
            finish(p)
            return
        table, step = (sums, number + 1) if number < 4 else (gathers, number - 3)
        for hh in range(2):
            getattr(table[p, hh], f"step{step}")()

    compute(0)
    pl.semaphore_wait(barrier, len(others))
    compute(1)
    for action, *which in SCHEDULE:
        {"compute": compute, "apply": apply, "stage": stage}[action](*which)

    for item in sums.values():
        for copy in item.sent:
            copy.wait_send()

    three = 3 * LOCAL
    token_copies = []
    other = pl.ds(pl.multiple_of((1 - head) * LOCAL, LOCAL), LOCAL)
    ours = pl.ds(pl.multiple_of(head * LOCAL, LOCAL), LOCAL)

    def token_part(r, which):
        return lax.dot_general(
            both[r * COLS:(r + 1) * COLS, :three], weights[which, :], NT,
            preferred_element_type=F32,
        )

    for r in range(ROWS):
        parts[0, r // 2, r % 2, :, :LOCAL] = token_part(r, other).astype(BF16)
        for q in range(4):
            rows = pl.ds(q * 128, 128)
            copy = remote(
                parts.at[0, r // 2, r % 2, rows, pl.ds(0, LOCAL)], arrived.at[r, rows, :],
                token_send, token_recv, (r, q), head_partner,
            )
            copy.start()
            token_copies.append(copy)

    weight_part(0, 0, LOCAL, tok, 2 * LOCAL)
    weight_part(0, LOCAL, LOCAL, cot, 3 * LOCAL)
    core_start(0)
    weight_part(1, 0, 2 * LOCAL, tok, 0)
    core_start(1)
    core_finish(0)
    weight_sums[0].step1()
    core_finish(1)
    weight_sums[1].step1()

    outs = []
    last = ROWS - 1

    def token_finish(r):
        here = last_own[...] if r == last else token_part(r, ours)
        for copy in token_copies[4 * r:4 * r + 4]:
            copy.wait_recv()
        parts[1, r // 2, r % 2, :, :LOCAL] = (arrived[r].astype(F32) + here).astype(BF16)
        copy = pltpu.make_async_copy(
            parts.at[1, r // 2, r % 2, :, pl.ds(0, LOCAL)], token_out.at[r], store.at[r]
        )
        copy.start()
        outs.append(copy)

    def weight_step(name):
        for item in weight_sums:
            getattr(item, name)()

    last_own[...] = token_part(last, ours)
    weight_step("step2")
    token_finish(0)
    weight_step("step3")
    weight_step("step4")
    token_finish(1)
    total = weight_sums[0].finish()[:12]
    weight_out[:, 2, :] = total[:, :LOCAL]
    weight_out[:, 3, :] = total[:, LOCAL:]
    total = weight_sums[1].finish()[:12]
    for p in range(PAIRS):
        for k in range(2):
            weight_out[:, k, p * PAIR:(p + 1) * PAIR] = (
                total[:, (2 * p + k) * PAIR:(2 * p + k + 1) * PAIR]
            )
    for r in range(2, ROWS):
        token_finish(r)

    for item in list(gathers.values()) + weight_sums:
        for copy in item.sent:
            copy.wait_send()
    for copy in token_copies + list(core_copies.values()):
        copy.wait_send()
    for copy in outs:
        copy.wait()


def local(tokens, w_query, w_key, w_value, w_out, cotangent):
    leading, rows_here, columns, model_width = tokens.shape
    scaling = 1.0 / math.sqrt(HDIM * rows_here * lax.axis_size("row"))
    anywhere = pl.BlockSpec(memory_space=pl.ANY)
    dma = pltpu.SemaphoreType.DMA
    wide = pltpu.VMEM((PAIRS, COLS, WIDE), BF16)
    inputs = pltpu.VMEM((ROWS * COLS, D), BF16)

    token_grads, weight_grads = pl.pallas_call(
        functools.partial(backward_kernel, scaling),
        out_shape=(
            jax.ShapeDtypeStruct((ROWS, COLS, LOCAL), BF16),
            jax.ShapeDtypeStruct((12, 4, LOCAL), F32),
        ),
        in_specs=[anywhere] * 6,
        out_specs=(anywhere, pl.BlockSpec(memory_space=pltpu.VMEM)),
        scratch_shapes=[
            inputs,
            inputs,
            pltpu.VMEM((D, 3 * LOCAL), BF16),
            pltpu.VMEM((LOCAL, D), BF16),
            wide,
            wide,
            wide,
            wide,
            pltpu.VMEM((2, PAIRS, 2, COLS, COLS), BF16),
            pltpu.VMEM((2, PAIRS, 2, 496, COLS), BF16),
            pltpu.VMEM((2, PAIRS, 2, COLS, COLS), BF16),
            pltpu.VMEM((ROWS * COLS, 4 * LOCAL), BF16),
            pltpu.VMEM((ROWS, COLS, LOCAL), BF16),
            pltpu.VMEM((2, LOCAL, 2 * LOCAL), BF16),
            pltpu.VMEM((2, 496, 2 * LOCAL), BF16),
            pltpu.VMEM((2, LOCAL + 8, 2 * LOCAL), F32),
            pltpu.VMEM((COLS, LOCAL), F32),
            dma((2, PAIRS, 16)),
            dma((2, PAIRS, 16)),
            dma((15,)),
            dma((ROWS, 4)),
            dma((ROWS, 4)),
            dma((2,)),
            dma((2,)),
            dma((2, 11)),
            dma((2, 11)),
            dma((ROWS,)),
        ],
        compiler_params=pltpu.CompilerParams(
            collective_id=0, has_side_effects=True, vmem_limit_bytes=63 * 2**20
        ),
        cost_estimate=pl.CostEstimate(
            flops=27 * 10**9, bytes_accessed=16 * 10**6, transcendentals=10**6
        ),
        name="row_attention_backward",
    )(
        tokens.reshape(-1, model_width), cotangent.reshape(-1, model_width),
        w_query, w_key, w_value, w_out,
    )

    return token_grads.reshape(leading, rows_here, columns, LOCAL), weight_grads


def solution(mesh):
    return jax.shard_map(
        local,
        mesh=mesh,
        in_specs=(
            P("aln", "row", None, None),
            P(None, "head"),
            P(None, "head"),
            P(None, "head"),
            P("head", None),
            P("aln", "row", None, None),
        ),
        out_specs=(P("aln", "row", None, "head"), P(("aln", "row"), None, "head")),
        check_vma=False,
    )
```

```python
import functools
import math

import jax
import jax.numpy as jnp
from jax import lax
from jax.experimental import pallas as pl
from jax.experimental.pallas import tpu as pltpu
from jax.sharding import PartitionSpec as P

HDIM = 64
MESH = pl.DeviceIdType.MESH
F32 = jnp.float32
BF16 = jnp.bfloat16

ROWS = 6
COLS = 512
D = 768
LOCAL = 384
PAIRS = 3
PAIR = 128
WIDE = ROWS * PAIR

NT = (((1,), (1,)), ((), ()))
TN = (((0,), (0,)), ((), ()))

SCHEDULE = (
    ("stage", 0, 0), ("compute", 2), ("stage", 0, 1), ("compute", 3),
    ("stage", 1, 0), ("compute", 4), ("stage", 0, 2), ("stage", 1, 1), ("compute", 5),
    ("stage", 2, 0), ("stage", 0, 3), ("stage", 1, 2),
    ("stage", 2, 1), ("stage", 0, 4), ("stage", 1, 3),
    ("stage", 0, 5), ("stage", 1, 4), ("stage", 0, 6),
    ("stage", 2, 2), ("stage", 1, 5), ("stage", 0, 7),
    ("stage", 2, 3), ("stage", 1, 6), ("stage", 0, 8),
    ("stage", 2, 4), ("stage", 1, 7), ("apply", 0),
    ("stage", 2, 5), ("apply", 1),
    ("stage", 2, 6), ("stage", 1, 8), ("apply", 2),
    ("stage", 2, 7), ("apply", 3),
    ("stage", 2, 8),
)


def position():
    row = lax.axis_index("row")
    return row // 8, (row // 2) % 4, row % 2


class Way:
    def __init__(self, place, ring, across, others, low, partner):
        self.place, (self.after, self.before) = place, ring
        self.across, self.others = across, others
        self.low, self.partner = low, partner


def neighbours():
    z, x, low = position()

    def at(z, x, low):
        return (lax.axis_index("aln"), z * 8 + x * 2 + low, lax.axis_index("head"))

    far = (2, 1, 3)
    z_ring = [at((z + d) % 4, x, low) for d in far]
    x_ring = [at(z, (x + d) % 4, low) for d in far]
    partner = at(z, x, 1 - low)
    z_others = [((z + d) % 4, device) for d, device in zip(far, z_ring)]
    x_others = [((x + d) % 4, device) for d, device in zip(far, x_ring)]
    return (
        Way(z, z_ring[1:], x, x_others, low, partner),
        Way(x, x_ring[1:], z, z_others, low, partner),
    )


def remote(src, dst, send, recv, index, device):
    return pltpu.make_async_remote_copy(
        src_ref=src,
        dst_ref=dst,
        send_sem=send.at[index],
        recv_sem=recv.at[index],
        device_id=device,
        device_id_type=MESH,
    )


class Transfers:
    def __init__(self, send, recv, base, way):
        self.send, self.recv, self.base, self.way = send, recv, base, way
        self.pending = []
        self.later = []
        self.sent = []

    def go(self, source, landing, slot, device, late=False):
        copy = remote(source, landing, self.send, self.recv, self.base + (slot,), device)
        copy.start()
        (self.later if late else self.pending).append(copy)
        self.sent.append(copy)

    def arrive(self):
        for copy in self.pending:
            copy.wait_recv()
        self.pending, self.later = self.later, []

    def block(self, step):
        return ((self.way.place + step) % 4) * 128

    def half(self, low):
        return self.block(0) + low * 64

    def own(self):
        return self.half(self.way.low) + self.way.across * 16


class Sum(Transfers):
    def __init__(self, part, got, *rest, late=False):
        super().__init__(*rest)
        self.part, self.got, self.late = part, got, late

    def add(self, at, size, *landings):
        total = self.part(at, size)[...].astype(F32)
        for landing in landings:
            total = total + self.got(landing, size)[...].astype(F32)
        return total

    def put(self, at, size, *landings):
        self.part(at, size)[...] = self.add(at, size, *landings).astype(BF16)

    def step1(self):
        far = self.block(2)
        self.go(self.part(far, 64), self.got(0, 64), 0, self.way.after)
        self.go(self.part(far + 64, 64), self.got(64, 64), 1, self.way.before)
        up, down = self.block(1), self.block(3)
        self.go(self.part(up + 64, 64), self.got(192, 64), 2, self.way.after, late=True)
        self.go(self.part(down, 64), self.got(256, 64), 3, self.way.before, late=True)

    def step2(self):
        self.arrive()
        up, down = self.block(1), self.block(3) + 64
        self.put(up, 64, 0)
        self.go(self.part(up, 64), self.got(128, 64), 4, self.way.after)
        self.put(down, 64, 64)
        self.go(self.part(down, 64), self.got(320, 64), 5, self.way.before)

    def step3(self):
        self.arrive()
        self.put(self.block(0), 128, 128, 256)
        low = self.way.low
        if self.late:
            for j, (place, device) in enumerate(self.way.others):
                for k, which in enumerate((low, 1 - low)):
                    self.go(
                        self.part(self.half(which) + place * 16, 16),
                        self.got(384 + 48 * k + 16 * j, 16), 6 + 3 * k + j, device,
                    )
        else:
            self.go(self.part(self.half(1 - low), 64), self.got(384, 64), 6, self.way.partner)

    def step4(self):
        self.arrive()
        low = self.way.low
        if self.late:
            there = self.half(1 - low) + self.way.across * 16
            self.put(there, 16, 432, 448, 464)
            self.go(self.part(there, 16), self.got(480, 16), 12, self.way.partner)
            return
        self.put(self.half(low), 64, 384)
        for j, (place, device) in enumerate(self.way.others):
            self.go(
                self.part(self.half(low) + place * 16, 16), self.got(448 + 16 * j, 16),
                7 + j, device,
            )

    def finish(self):
        self.arrive()
        landings = (384, 400, 416, 480) if self.late else (448, 464, 480)
        return self.add(self.own(), 16, *landings)


class Gather(Transfers):
    def __init__(self, part, *rest):
        super().__init__(*rest)
        self.part = part

    def same(self, at, size, slot, device, late=False):
        self.go(self.part(at, size), self.part(at, size), slot, device, late)

    def step1(self):
        for j, (_, device) in enumerate(self.way.others):
            self.same(self.own(), 16, 10 + j, device)

    def step2(self):
        self.arrive()
        self.same(self.half(self.way.low), 64, 13, self.way.partner)

    def step3(self):
        self.arrive()
        here = self.block(0)
        self.same(here, 64, 14, self.way.after)
        self.same(here + 64, 64, 15, self.way.before)
        self.same(here + 64, 64, 16, self.way.after, late=True)
        self.same(here, 64, 17, self.way.before, late=True)

    def step4(self):
        self.arrive()
        self.same(self.block(3), 64, 18, self.way.after)
        self.same(self.block(1) + 64, 64, 19, self.way.before)

    def step5(self):
        self.arrive()


def rows_of(ref, *lead):
    def view(start, size):
        at = start if isinstance(start, int) else pl.multiple_of(start, 16)
        return ref.at[(*lead, pl.ds(at, size), slice(None))]

    return view


def backward_kernel(
    scaling,
    tokens, cotangent, w_query, w_key, w_value, w_out,
    token_out, weight_out,
    tok, cot, weights, wo, queries, keys, values, outgrads,
    parts, landed, maps, both, arrived, core_arrived, weight_landed, mine, last_own,
    send, recv, load, token_send, token_recv, core_send, core_recv,
    weight_send, weight_recv, store,
):
    ways = neighbours()
    aln, row, head = lax.axis_index("aln"), lax.axis_index("row"), lax.axis_index("head")
    head_partner = (aln, row, 1 - head)
    core_partner = (1 - aln, row, head)

    loads = []

    def fetch(src, dst):
        copy = pltpu.make_async_copy(src, dst, load.at[len(loads)])
        copy.start()
        loads.append(copy)
        return copy

    need = {u: [] for u in range(2 * PAIRS)}
    for p in range(PAIRS):
        lanes = pl.ds(p * PAIR, PAIR)
        need[2 * p].append(
            fetch(w_query.at[:, lanes], weights.at[:, pl.ds(2 * p * PAIR, PAIR)])
        )
        need[2 * p].append(
            fetch(w_key.at[:, lanes], weights.at[:, pl.ds((2 * p + 1) * PAIR, PAIR)])
        )
        if p == 0:
            token_loads = [
                fetch(tokens.at[pl.ds(r * COLS, COLS), :], tok.at[pl.ds(r * COLS, COLS), :])
                for r in range(ROWS)
            ]
            need[1].append(fetch(cotangent, cot))
            need[1].append(fetch(w_value, weights.at[:, pl.ds(2 * LOCAL, LOCAL)]))
            need[1].append(fetch(w_out, wo))

    barrier = pltpu.get_barrier_semaphore()
    others = [device for way in ways for _, device in way.others]
    others += [ways[0].partner, head_partner, core_partner]
    for device in others:
        pl.semaphore_signal(barrier, inc=1, device_id=device, device_id_type=MESH)

    lane = lax.broadcasted_iota(jnp.int32, (1, WIDE), 1)
    even = ((lane % PAIR) < HDIM).astype(F32)
    masks = [even.astype(BF16), (1.0 - even).astype(BF16)]

    sums, gathers = {}, {}
    for p in range(PAIRS):
        for hh in range(2):
            lead = (hh, p, slice(None))
            sums[p, hh] = Sum(
                rows_of(parts, *lead), rows_of(landed, *lead), send, recv, (hh, p), ways[hh]
            )
            gathers[p, hh] = Gather(rows_of(maps, *lead), send, recv, (hh, p), ways[hh])

    def project(p, size, first):
        rows = pl.ds(first * COLS, 3 * COLS)
        if size is None:
            out = jnp.dot(
                tok[rows, :], weights[:, 2 * p * PAIR:2 * (p + 1) * PAIR],
                preferred_element_type=F32,
            ).astype(BF16)
            targets = ((queries, p, out[:, :PAIR]), (keys, p, out[:, PAIR:]))
        else:
            value = jnp.dot(
                tok[rows, :],
                weights[:, 2 * LOCAL + p * PAIR:2 * LOCAL + (p + size) * PAIR],
                preferred_element_type=F32,
            ).astype(BF16)
            outgrad = lax.dot_general(
                cot[rows, :], wo[p * PAIR:(p + size) * PAIR, :], NT,
                preferred_element_type=F32,
            ).astype(BF16)
            targets = []
            for q in range(size):
                lanes = slice(q * PAIR, (q + 1) * PAIR)
                targets += [(values, p + q, value[:, lanes]), (outgrads, p + q, outgrad[:, lanes])]
        for ref, at, out in targets:
            for r in range(3):
                lanes = slice((first + r) * PAIR, (first + r + 1) * PAIR)
                ref[at, :, lanes] = out[r * COLS:(r + 1) * COLS, :]

    def compute(u):
        p, kind = u // 2, u % 2
        for copy in need[u]:
            copy.wait()
        size = None if kind == 0 else {0: 2, 1: 0, 2: 1}[p]
        if size != 0:
            for first in (0, 3):
                if u == 0:
                    for r in range(3):
                        token_loads[first + r].wait()
                project(p, size, first)
        left, right = (queries, keys) if kind == 0 else (outgrads, values)
        for hh in range(2):
            masked = right[p] * masks[hh]
            for b in range(2):
                rows = pl.ds(b * 256, 256)
                parts[hh, p, kind, rows, :] = lax.dot_general(
                    left[p, rows, :], masked, NT, preferred_element_type=F32
                ).astype(BF16)

    def finish(p):
        for hh in range(2):
            total = sums[p, hh].finish()
            rows = pl.ds(pl.multiple_of(sums[p, hh].own(), 16), 16)
            scores = total[0] * scaling
            powers = jnp.exp(scores - jnp.max(scores, axis=-1, keepdims=True))
            attention = (powers / jnp.sum(powers, axis=-1, keepdims=True)).astype(BF16)
            maps[hh, p, 0, rows, :] = attention
            attention = attention.astype(F32)
            centre = jnp.sum(attention * total[1], axis=-1, keepdims=True)
            maps[hh, p, 1, rows, :] = (attention * (total[1] - centre) * scaling).astype(BF16)
            gathers[p, hh].step1()

    def emit(lane_at, b, first, value):
        value = value.astype(BF16)
        for r in range(value.shape[1] // PAIR):
            at = (first + r) * COLS + b * 256
            both[at:at + 256, lane_at:lane_at + PAIR] = value[:, r * PAIR:(r + 1) * PAIR]

    def apply_ahead(u, first=0, count=ROWS):
        p, kind = u // 2, u % 2
        source, lane_at = ((values, 3 * LOCAL + p * PAIR), (keys, 2 * p * PAIR))[kind]
        lanes = slice(first * PAIR, (first + count) * PAIR)
        ahead = [source[p, :, lanes] * masks[hh][:, lanes] for hh in range(2)]
        for b in range(2):
            rows = pl.ds(b * 256, 256)
            out = jnp.dot(maps[0, p, kind, rows, :], ahead[0], preferred_element_type=F32)
            out = out + jnp.dot(maps[1, p, kind, rows, :], ahead[1], preferred_element_type=F32)
            emit(lane_at, b, first, out)

    def apply_back(u, first=0, count=ROWS):
        p, kind = u // 2, u % 2
        source, lane_at = (
            (outgrads, 2 * LOCAL + p * PAIR), (queries, (2 * p + 1) * PAIR)
        )[kind]
        lanes = slice(first * PAIR, (first + count) * PAIR)
        back = [source[p, :, lanes] * masks[hh][:, lanes] for hh in range(2)]
        for b in range(2):
            rows = pl.ds(b * 256, 256)
            out = lax.dot_general(
                maps[0, p, kind, :, rows], back[0], TN, preferred_element_type=F32
            )
            out = out + lax.dot_general(
                maps[1, p, kind, :, rows], back[1], TN, preferred_element_type=F32
            )
            emit(lane_at, b, first, out)

    def apply(u):
        apply_ahead(u)
        apply_back(u)

    other_lanes = pl.ds(pl.multiple_of((1 - aln) * LOCAL, LOCAL), LOCAL)
    own_lanes = pl.ds(pl.multiple_of(aln * LOCAL, LOCAL), LOCAL)

    def weight_part(part, lane_at, size, source, column):
        right = pl.ds(column, size)
        queries[part, pl.ds(0, LOCAL), pl.ds(lane_at, size)] = lax.dot_general(
            source[:, other_lanes], both[:, right], TN, preferred_element_type=F32
        ).astype(BF16)
        mine[part, pl.ds(0, LOCAL), pl.ds(lane_at, size)] = lax.dot_general(
            source[:, own_lanes], both[:, right], TN, preferred_element_type=F32
        )

    core_copies = {}

    def core_start(part):
        core_copies[part] = remote(
            queries.at[part, pl.ds(0, LOCAL), :], core_arrived.at[part],
            core_send, core_recv, (part,), core_partner,
        )
        core_copies[part].start()

    weight_sums = [
        Sum(
            rows_of(keys, part), rows_of(weight_landed, part), weight_send, weight_recv,
            (part,), way, late=True,
        )
        for part, way in enumerate(ways)
    ]

    def core_finish(part):
        core_copies[part].wait_recv()
        mine[part, pl.ds(0, LOCAL), :] += core_arrived[part].astype(F32)
        mine[part, pl.ds(LOCAL, 8), :] = jnp.zeros((8, 2 * LOCAL), F32)
        for z in range(4):
            for x in range(4):
                for low in range(2):
                    at = (z * 128 + x * 16, x * 128 + z * 16)[part] + low * 64
                    keys[part, at:at + 16, :] = mine[
                        part, pl.ds((z * 8 + x * 2 + low) * 12, 16), :
                    ].astype(BF16)

    def stage(p, number):
        if number == 4:
            finish(p)
            return
        table, step = (sums, number + 1) if number < 4 else (gathers, number - 3)
        for hh in range(2):
            getattr(table[p, hh], f"step{step}")()

    compute(0)
    pl.semaphore_wait(barrier, len(others))
    compute(1)
    for action, *which in SCHEDULE:
        {"compute": compute, "apply": apply, "stage": stage}[action](*which)

    for item in sums.values():
        for copy in item.sent:
            copy.wait_send()

    three = 3 * LOCAL
    token_copies = []
    other = pl.ds(pl.multiple_of((1 - head) * LOCAL, LOCAL), LOCAL)
    ours = pl.ds(pl.multiple_of(head * LOCAL, LOCAL), LOCAL)

    def token_part(r, which):
        return lax.dot_general(
            both[r * COLS:(r + 1) * COLS, :three], weights[which, :], NT,
            preferred_element_type=F32,
        )

    for r in range(ROWS):
        if r % 2 == 0:
            apply_back(4, r, 2)
            apply_ahead(5, r, 2)
            apply_back(5, r, 2)
        parts[0, r // 2, r % 2, :, :LOCAL] = token_part(r, other).astype(BF16)
        for q in range(4):
            rows = pl.ds(q * 128, 128)
            copy = remote(
                parts.at[0, r // 2, r % 2, rows, pl.ds(0, LOCAL)], arrived.at[r, rows, :],
                token_send, token_recv, (r, q), head_partner,
            )
            copy.start()
            token_copies.append(copy)

    apply_ahead(4)
    weight_part(0, 0, LOCAL, tok, 2 * LOCAL)
    weight_part(0, LOCAL, LOCAL, cot, 3 * LOCAL)
    core_start(0)
    weight_part(1, 0, 2 * LOCAL, tok, 0)
    core_start(1)
    core_finish(0)
    weight_sums[0].step1()
    core_finish(1)
    weight_sums[1].step1()

    outs = []
    last = ROWS - 1

    def token_finish(r):
        here = last_own[...] if r == last else token_part(r, ours)
        for copy in token_copies[4 * r:4 * r + 4]:
            copy.wait_recv()
        parts[1, r // 2, r % 2, :, :LOCAL] = (arrived[r].astype(F32) + here).astype(BF16)
        copy = pltpu.make_async_copy(
            parts.at[1, r // 2, r % 2, :, pl.ds(0, LOCAL)], token_out.at[r], store.at[r]
        )
        copy.start()
        outs.append(copy)

    def weight_step(name):
        for item in weight_sums:
            getattr(item, name)()

    last_own[...] = token_part(last, ours)
    weight_step("step2")
    token_finish(0)
    weight_step("step3")
    weight_step("step4")
    token_finish(1)
    total = weight_sums[0].finish()[:12]
    weight_out[:, 2, :] = total[:, :LOCAL]
    weight_out[:, 3, :] = total[:, LOCAL:]
    total = weight_sums[1].finish()[:12]
    for p in range(PAIRS):
        for k in range(2):
            weight_out[:, k, p * PAIR:(p + 1) * PAIR] = (
                total[:, (2 * p + k) * PAIR:(2 * p + k + 1) * PAIR]
            )
    for r in range(2, ROWS):
        token_finish(r)

    for item in list(gathers.values()) + weight_sums:
        for copy in item.sent:
            copy.wait_send()
    for copy in token_copies + list(core_copies.values()):
        copy.wait_send()
    for copy in outs:
        copy.wait()


def local(tokens, w_query, w_key, w_value, w_out, cotangent):
    leading, rows_here, columns, model_width = tokens.shape
    scaling = 1.0 / math.sqrt(HDIM * rows_here * lax.axis_size("row"))
    anywhere = pl.BlockSpec(memory_space=pl.ANY)
    dma = pltpu.SemaphoreType.DMA
    wide = pltpu.VMEM((PAIRS, COLS, WIDE), BF16)
    inputs = pltpu.VMEM((ROWS * COLS, D), BF16)

    token_grads, weight_grads = pl.pallas_call(
        functools.partial(backward_kernel, scaling),
        out_shape=(
            jax.ShapeDtypeStruct((ROWS, COLS, LOCAL), BF16),
            jax.ShapeDtypeStruct((12, 4, LOCAL), F32),
        ),
        in_specs=[anywhere] * 6,
        out_specs=(anywhere, pl.BlockSpec(memory_space=pltpu.VMEM)),
        scratch_shapes=[
            inputs,
            inputs,
            pltpu.VMEM((D, 3 * LOCAL), BF16),
            pltpu.VMEM((LOCAL, D), BF16),
            wide,
            wide,
            wide,
            wide,
            pltpu.VMEM((2, PAIRS, 2, COLS, COLS), BF16),
            pltpu.VMEM((2, PAIRS, 2, 496, COLS), BF16),
            pltpu.VMEM((2, PAIRS, 2, COLS, COLS), BF16),
            pltpu.VMEM((ROWS * COLS, 4 * LOCAL), BF16),
            pltpu.VMEM((ROWS, COLS, LOCAL), BF16),
            pltpu.VMEM((2, LOCAL, 2 * LOCAL), BF16),
            pltpu.VMEM((2, 496, 2 * LOCAL), BF16),
            pltpu.VMEM((2, LOCAL + 8, 2 * LOCAL), F32),
            pltpu.VMEM((COLS, LOCAL), F32),
            dma((2, PAIRS, 20)),
            dma((2, PAIRS, 20)),
            dma((15,)),
            dma((ROWS, 4)),
            dma((ROWS, 4)),
            dma((2,)),
            dma((2,)),
            dma((2, 13)),
            dma((2, 13)),
            dma((ROWS,)),
        ],
        compiler_params=pltpu.CompilerParams(
            collective_id=0, has_side_effects=True, vmem_limit_bytes=63 * 2**20
        ),
        cost_estimate=pl.CostEstimate(
            flops=27 * 10**9, bytes_accessed=16 * 10**6, transcendentals=10**6
        ),
        name="row_attention_backward",
    )(
        tokens.reshape(-1, model_width), cotangent.reshape(-1, model_width),
        w_query, w_key, w_value, w_out,
    )

    return token_grads.reshape(leading, rows_here, columns, LOCAL), weight_grads


def solution(mesh):
    return jax.shard_map(
        local,
        mesh=mesh,
        in_specs=(
            P("aln", "row", None, None),
            P(None, "head"),
            P(None, "head"),
            P(None, "head"),
            P("head", None),
            P("aln", "row", None, None),
        ),
        out_specs=(P("aln", "row", None, "head"), P(("aln", "row"), None, "head")),
        check_vma=False,
    )
```

```python
import functools
import math

import jax
import jax.numpy as jnp
from jax import lax
from jax.experimental import pallas as pl
from jax.experimental.pallas import tpu as pltpu
from jax.sharding import PartitionSpec as P

HDIM = 64
MESH = pl.DeviceIdType.MESH
F32 = jnp.float32
BF16 = jnp.bfloat16

ROWS = 6
COLS = 512
D = 768
LOCAL = 384
PAIRS = 3
PAIR = 128
WIDE = ROWS * PAIR

NT = (((1,), (1,)), ((), ()))
TN = (((0,), (0,)), ((), ()))

SCHEDULE = (
    ("stage", 0, 0), ("compute", 2), ("stage", 0, 1), ("compute", 3),
    ("stage", 1, 0), ("compute", 4), ("stage", 0, 2), ("stage", 1, 1), ("compute", 5),
    ("stage", 2, 0), ("stage", 0, 3), ("stage", 1, 2),
    ("stage", 2, 1), ("stage", 0, 4), ("stage", 1, 3),
    ("stage", 2, 2), ("stage", 0, 5), ("stage", 1, 4),
    ("stage", 2, 3), ("stage", 0, 6), ("stage", 1, 5),
    ("stage", 2, 4), ("stage", 0, 7), ("stage", 1, 6),
    ("stage", 2, 5), ("stage", 0, 8), ("apply", 0),
    ("stage", 2, 6), ("stage", 1, 7), ("apply", 1),
    ("stage", 2, 7), ("stage", 1, 8), ("apply", 2), ("apply", 3),
    ("stage", 2, 8),
)


def position():
    row = lax.axis_index("row")
    return row // 8, (row // 2) % 4, row % 2


class Way:
    def __init__(self, place, ring, across, others, low, partner):
        self.place, (self.after, self.before) = place, ring
        self.across, self.others = across, others
        self.low, self.partner = low, partner


def neighbours():
    z, x, low = position()

    def at(z, x, low):
        return (lax.axis_index("aln"), z * 8 + x * 2 + low, lax.axis_index("head"))

    far = (2, 1, 3)
    z_ring = [at((z + d) % 4, x, low) for d in far]
    x_ring = [at(z, (x + d) % 4, low) for d in far]
    partner = at(z, x, 1 - low)
    z_others = [((z + d) % 4, device) for d, device in zip(far, z_ring)]
    x_others = [((x + d) % 4, device) for d, device in zip(far, x_ring)]
    return (
        Way(z, z_ring[1:], x, x_others, low, partner),
        Way(x, x_ring[1:], z, z_others, low, partner),
    )


def remote(src, dst, send, recv, index, device):
    return pltpu.make_async_remote_copy(
        src_ref=src,
        dst_ref=dst,
        send_sem=send.at[index],
        recv_sem=recv.at[index],
        device_id=device,
        device_id_type=MESH,
    )


class Transfers:
    def __init__(self, send, recv, base, way):
        self.send, self.recv, self.base, self.way = send, recv, base, way
        self.pending = []
        self.later = []
        self.sent = []

    def go(self, source, landing, slot, device, late=False):
        copy = remote(source, landing, self.send, self.recv, self.base + (slot,), device)
        copy.start()
        (self.later if late else self.pending).append(copy)
        self.sent.append(copy)

    def arrive(self):
        for copy in self.pending:
            copy.wait_recv()
        self.pending, self.later = self.later, []

    def block(self, step):
        return ((self.way.place + step) % 4) * 128

    def half(self, low):
        return self.block(0) + low * 64

    def own(self):
        return self.half(self.way.low) + self.way.across * 16


class Sum(Transfers):
    def __init__(self, part, got, *rest, late=False):
        super().__init__(*rest)
        self.part, self.got, self.late = part, got, late

    def add(self, at, size, *landings):
        total = self.part(at, size)[...].astype(F32)
        for landing in landings:
            total = total + self.got(landing, size)[...].astype(F32)
        return total

    def put(self, at, size, *landings):
        self.part(at, size)[...] = self.add(at, size, *landings).astype(BF16)

    def step1(self):
        far = self.block(2)
        self.go(self.part(far, 64), self.got(0, 64), 0, self.way.after)
        self.go(self.part(far + 64, 64), self.got(64, 64), 1, self.way.before)
        up, down = self.block(1), self.block(3)
        self.go(self.part(up + 64, 64), self.got(192, 64), 2, self.way.after, late=True)
        self.go(self.part(down, 64), self.got(256, 64), 3, self.way.before, late=True)

    def step2(self):
        self.arrive()
        up, down = self.block(1), self.block(3) + 64
        self.put(up, 64, 0)
        self.go(self.part(up, 64), self.got(128, 64), 4, self.way.after)
        self.put(down, 64, 64)
        self.go(self.part(down, 64), self.got(320, 64), 5, self.way.before)

    def step3(self):
        self.arrive()
        self.put(self.block(0), 128, 128, 256)
        low = self.way.low
        if self.late:
            for j, (place, device) in enumerate(self.way.others):
                for k, which in enumerate((low, 1 - low)):
                    self.go(
                        self.part(self.half(which) + place * 16, 16),
                        self.got(384 + 48 * k + 16 * j, 16), 6 + 3 * k + j, device,
                    )
        else:
            self.go(self.part(self.half(1 - low), 64), self.got(384, 64), 6, self.way.partner)

    def step4(self):
        self.arrive()
        low = self.way.low
        if self.late:
            there = self.half(1 - low) + self.way.across * 16
            self.put(there, 16, 432, 448, 464)
            self.go(self.part(there, 16), self.got(480, 16), 12, self.way.partner)
            return
        self.put(self.half(low), 64, 384)
        for j, (place, device) in enumerate(self.way.others):
            self.go(
                self.part(self.half(low) + place * 16, 16), self.got(448 + 16 * j, 16),
                7 + j, device,
            )

    def finish(self):
        self.arrive()
        landings = (384, 400, 416, 480) if self.late else (448, 464, 480)
        return self.add(self.own(), 16, *landings)


class Gather(Transfers):
    def __init__(self, part, *rest, late=False):
        super().__init__(*rest)
        self.part, self.late = part, late

    def same(self, at, size, slot, device, late=False):
        self.go(self.part(at, size), self.part(at, size), slot, device, late)

    def step1(self):
        if self.late:
            self.same(self.own(), 16, 13, self.way.partner)
            return
        for j, (_, device) in enumerate(self.way.others):
            self.same(self.own(), 16, 13 + j, device)

    def step2(self):
        self.arrive()
        low = self.way.low
        if self.late:
            for j, (_, device) in enumerate(self.way.others):
                for k, which in enumerate((low, 1 - low)):
                    at = self.half(which) + self.way.across * 16
                    self.same(at, 16, 14 + 3 * k + j, device)
            return
        self.same(self.half(low), 64, 16, self.way.partner)

    def step3(self):
        self.arrive()
        here = self.block(0)
        self.same(here, 64, 20, self.way.after)
        self.same(here + 64, 64, 21, self.way.before)
        self.same(here + 64, 64, 22, self.way.after, late=True)
        self.same(here, 64, 23, self.way.before, late=True)

    def step4(self):
        self.arrive()
        self.same(self.block(3), 64, 24, self.way.after)
        self.same(self.block(1) + 64, 64, 25, self.way.before)

    def step5(self):
        self.arrive()


def rows_of(ref, *lead):
    def view(start, size):
        at = start if isinstance(start, int) else pl.multiple_of(start, 16)
        return ref.at[(*lead, pl.ds(at, size), slice(None))]

    return view


def backward_kernel(
    scaling,
    tokens, cotangent, w_query, w_key, w_value, w_out,
    token_out, weight_out,
    tok, cot, weights, wo, queries, keys, values, outgrads,
    parts, landed, maps, both, arrived, core_arrived, weight_landed, mine, last_own,
    send, recv, load, token_send, token_recv, core_send, core_recv,
    weight_send, weight_recv, store,
):
    ways = neighbours()
    aln, row, head = lax.axis_index("aln"), lax.axis_index("row"), lax.axis_index("head")
    head_partner = (aln, row, 1 - head)
    core_partner = (1 - aln, row, head)

    loads = []

    def fetch(src, dst):
        copy = pltpu.make_async_copy(src, dst, load.at[len(loads)])
        copy.start()
        loads.append(copy)
        return copy

    need = {u: [] for u in range(2 * PAIRS)}
    for p in range(PAIRS):
        lanes = pl.ds(p * PAIR, PAIR)
        need[2 * p].append(
            fetch(w_query.at[:, lanes], weights.at[:, pl.ds(2 * p * PAIR, PAIR)])
        )
        need[2 * p].append(
            fetch(w_key.at[:, lanes], weights.at[:, pl.ds((2 * p + 1) * PAIR, PAIR)])
        )
        if p == 0:
            token_loads = [
                fetch(tokens.at[pl.ds(r * COLS, COLS), :], tok.at[pl.ds(r * COLS, COLS), :])
                for r in range(ROWS)
            ]
            need[1].append(fetch(cotangent, cot))
            need[1].append(fetch(w_value, weights.at[:, pl.ds(2 * LOCAL, LOCAL)]))
            need[1].append(fetch(w_out, wo))

    barrier = pltpu.get_barrier_semaphore()
    others = [device for way in ways for _, device in way.others]
    others += [ways[0].partner, head_partner, core_partner]
    for device in others:
        pl.semaphore_signal(barrier, inc=1, device_id=device, device_id_type=MESH)

    lane = lax.broadcasted_iota(jnp.int32, (1, WIDE), 1)
    even = ((lane % PAIR) < HDIM).astype(F32)
    masks = [even.astype(BF16), (1.0 - even).astype(BF16)]

    sums, gathers = {}, {}
    for p in range(PAIRS):
        for hh in range(2):
            lead = (hh, p, slice(None))
            sums[p, hh] = Sum(
                rows_of(parts, *lead), rows_of(landed, *lead), send, recv, (hh, p), ways[hh],
                late=p == PAIRS - 1,
            )
            gathers[p, hh] = Gather(
                rows_of(maps, *lead), send, recv, (hh, p), ways[hh], late=p == PAIRS - 1
            )

    def project(p, size, first):
        rows = pl.ds(first * COLS, 3 * COLS)
        if size is None:
            out = jnp.dot(
                tok[rows, :], weights[:, 2 * p * PAIR:2 * (p + 1) * PAIR],
                preferred_element_type=F32,
            ).astype(BF16)
            targets = ((queries, p, out[:, :PAIR]), (keys, p, out[:, PAIR:]))
        else:
            value = jnp.dot(
                tok[rows, :],
                weights[:, 2 * LOCAL + p * PAIR:2 * LOCAL + (p + size) * PAIR],
                preferred_element_type=F32,
            ).astype(BF16)
            outgrad = lax.dot_general(
                cot[rows, :], wo[p * PAIR:(p + size) * PAIR, :], NT,
                preferred_element_type=F32,
            ).astype(BF16)
            targets = []
            for q in range(size):
                lanes = slice(q * PAIR, (q + 1) * PAIR)
                targets += [(values, p + q, value[:, lanes]), (outgrads, p + q, outgrad[:, lanes])]
        for ref, at, out in targets:
            for r in range(3):
                lanes = slice((first + r) * PAIR, (first + r + 1) * PAIR)
                ref[at, :, lanes] = out[r * COLS:(r + 1) * COLS, :]

    def compute(u):
        p, kind = u // 2, u % 2
        for copy in need[u]:
            copy.wait()
        size = None if kind == 0 else {0: 2, 1: 0, 2: 1}[p]
        if size != 0:
            for first in (0, 3):
                if u == 0:
                    for r in range(3):
                        token_loads[first + r].wait()
                project(p, size, first)
        left, right = (queries, keys) if kind == 0 else (outgrads, values)
        for hh in range(2):
            masked = right[p] * masks[hh]
            for b in range(2):
                rows = pl.ds(b * 256, 256)
                parts[hh, p, kind, rows, :] = lax.dot_general(
                    left[p, rows, :], masked, NT, preferred_element_type=F32
                ).astype(BF16)

    def finish(p):
        for hh in range(2):
            total = sums[p, hh].finish()
            rows = pl.ds(pl.multiple_of(sums[p, hh].own(), 16), 16)
            scores = total[0] * scaling
            powers = jnp.exp(scores - jnp.max(scores, axis=-1, keepdims=True))
            attention = (powers / jnp.sum(powers, axis=-1, keepdims=True)).astype(BF16)
            maps[hh, p, 0, rows, :] = attention
            attention = attention.astype(F32)
            centre = jnp.sum(attention * total[1], axis=-1, keepdims=True)
            maps[hh, p, 1, rows, :] = (attention * (total[1] - centre) * scaling).astype(BF16)
            gathers[p, hh].step1()

    def emit(lane_at, b, first, value):
        value = value.astype(BF16)
        for r in range(value.shape[1] // PAIR):
            at = (first + r) * COLS + b * 256
            both[at:at + 256, lane_at:lane_at + PAIR] = value[:, r * PAIR:(r + 1) * PAIR]

    def apply_ahead(u, first=0, count=ROWS):
        p, kind = u // 2, u % 2
        source, lane_at = ((values, 3 * LOCAL + p * PAIR), (keys, 2 * p * PAIR))[kind]
        lanes = slice(first * PAIR, (first + count) * PAIR)
        ahead = [source[p, :, lanes] * masks[hh][:, lanes] for hh in range(2)]
        for b in range(2):
            rows = pl.ds(b * 256, 256)
            out = jnp.dot(maps[0, p, kind, rows, :], ahead[0], preferred_element_type=F32)
            out = out + jnp.dot(maps[1, p, kind, rows, :], ahead[1], preferred_element_type=F32)
            emit(lane_at, b, first, out)

    def apply_back(u, first=0, count=ROWS):
        p, kind = u // 2, u % 2
        source, lane_at = (
            (outgrads, 2 * LOCAL + p * PAIR), (queries, (2 * p + 1) * PAIR)
        )[kind]
        lanes = slice(first * PAIR, (first + count) * PAIR)
        back = [source[p, :, lanes] * masks[hh][:, lanes] for hh in range(2)]
        for b in range(2):
            rows = pl.ds(b * 256, 256)
            out = lax.dot_general(
                maps[0, p, kind, :, rows], back[0], TN, preferred_element_type=F32
            )
            out = out + lax.dot_general(
                maps[1, p, kind, :, rows], back[1], TN, preferred_element_type=F32
            )
            emit(lane_at, b, first, out)

    def apply(u):
        apply_ahead(u)
        apply_back(u)

    other_lanes = pl.ds(pl.multiple_of((1 - aln) * LOCAL, LOCAL), LOCAL)
    own_lanes = pl.ds(pl.multiple_of(aln * LOCAL, LOCAL), LOCAL)

    def weight_part(part, lane_at, size, source, column):
        right = pl.ds(column, size)
        queries[part, pl.ds(0, LOCAL), pl.ds(lane_at, size)] = lax.dot_general(
            source[:, other_lanes], both[:, right], TN, preferred_element_type=F32
        ).astype(BF16)
        mine[part, pl.ds(0, LOCAL), pl.ds(lane_at, size)] = lax.dot_general(
            source[:, own_lanes], both[:, right], TN, preferred_element_type=F32
        )

    core_copies = {}

    def core_start(part):
        core_copies[part] = remote(
            queries.at[part, pl.ds(0, LOCAL), :], core_arrived.at[part],
            core_send, core_recv, (part,), core_partner,
        )
        core_copies[part].start()

    weight_sums = [
        Sum(
            rows_of(keys, part), rows_of(weight_landed, part), weight_send, weight_recv,
            (part,), way, late=True,
        )
        for part, way in enumerate(ways)
    ]

    def core_finish(part):
        core_copies[part].wait_recv()
        mine[part, pl.ds(0, LOCAL), :] += core_arrived[part].astype(F32)
        mine[part, pl.ds(LOCAL, 8), :] = jnp.zeros((8, 2 * LOCAL), F32)
        for z in range(4):
            for x in range(4):
                for low in range(2):
                    at = (z * 128 + x * 16, x * 128 + z * 16)[part] + low * 64
                    keys[part, at:at + 16, :] = mine[
                        part, pl.ds((z * 8 + x * 2 + low) * 12, 16), :
                    ].astype(BF16)

    def stage(p, number):
        if number == 4:
            finish(p)
            return
        table, step = (sums, number + 1) if number < 4 else (gathers, number - 3)
        for hh in range(2):
            getattr(table[p, hh], f"step{step}")()

    compute(0)
    pl.semaphore_wait(barrier, len(others))
    compute(1)
    for action, *which in SCHEDULE:
        {"compute": compute, "apply": apply, "stage": stage}[action](*which)

    for item in sums.values():
        for copy in item.sent:
            copy.wait_send()

    three = 3 * LOCAL
    token_copies = []
    other = pl.ds(pl.multiple_of((1 - head) * LOCAL, LOCAL), LOCAL)
    ours = pl.ds(pl.multiple_of(head * LOCAL, LOCAL), LOCAL)

    def token_part(r, which):
        return lax.dot_general(
            both[r * COLS:(r + 1) * COLS, :three], weights[which, :], NT,
            preferred_element_type=F32,
        )

    for r in range(ROWS):
        if r % 2 == 0:
            apply_back(4, r, 2)
            apply_ahead(5, r, 2)
            apply_back(5, r, 2)
        parts[0, r // 2, r % 2, :, :LOCAL] = token_part(r, other).astype(BF16)
        for q in range(4):
            rows = pl.ds(q * 128, 128)
            copy = remote(
                parts.at[0, r // 2, r % 2, rows, pl.ds(0, LOCAL)], arrived.at[r, rows, :],
                token_send, token_recv, (r, q), head_partner,
            )
            copy.start()
            token_copies.append(copy)

    apply_ahead(4)
    weight_part(0, 0, LOCAL, tok, 2 * LOCAL)
    weight_part(0, LOCAL, LOCAL, cot, 3 * LOCAL)
    core_start(0)
    weight_part(1, 0, 2 * LOCAL, tok, 0)
    core_start(1)
    core_finish(0)
    weight_sums[0].step1()
    core_finish(1)
    weight_sums[1].step1()

    outs = []
    last = ROWS - 1

    def token_finish(r):
        here = last_own[...] if r == last else token_part(r, ours)
        for copy in token_copies[4 * r:4 * r + 4]:
            copy.wait_recv()
        parts[1, r // 2, r % 2, :, :LOCAL] = (arrived[r].astype(F32) + here).astype(BF16)
        copy = pltpu.make_async_copy(
            parts.at[1, r // 2, r % 2, :, pl.ds(0, LOCAL)], token_out.at[r], store.at[r]
        )
        copy.start()
        outs.append(copy)

    def weight_step(name):
        for item in weight_sums:
            getattr(item, name)()

    last_own[...] = token_part(last, ours)
    weight_step("step2")
    token_finish(0)
    weight_step("step3")
    weight_step("step4")
    token_finish(1)
    total = weight_sums[0].finish()[:12]
    weight_out[:, 2, :] = total[:, :LOCAL]
    weight_out[:, 3, :] = total[:, LOCAL:]
    total = weight_sums[1].finish()[:12]
    for p in range(PAIRS):
        for k in range(2):
            weight_out[:, k, p * PAIR:(p + 1) * PAIR] = (
                total[:, (2 * p + k) * PAIR:(2 * p + k + 1) * PAIR]
            )
    for r in range(2, ROWS):
        token_finish(r)

    for item in list(gathers.values()) + weight_sums:
        for copy in item.sent:
            copy.wait_send()
    for copy in token_copies + list(core_copies.values()):
        copy.wait_send()
    for copy in outs:
        copy.wait()


def local(tokens, w_query, w_key, w_value, w_out, cotangent):
    leading, rows_here, columns, model_width = tokens.shape
    scaling = 1.0 / math.sqrt(HDIM * rows_here * lax.axis_size("row"))
    anywhere = pl.BlockSpec(memory_space=pl.ANY)
    dma = pltpu.SemaphoreType.DMA
    wide = pltpu.VMEM((PAIRS, COLS, WIDE), BF16)
    inputs = pltpu.VMEM((ROWS * COLS, D), BF16)

    token_grads, weight_grads = pl.pallas_call(
        functools.partial(backward_kernel, scaling),
        out_shape=(
            jax.ShapeDtypeStruct((ROWS, COLS, LOCAL), BF16),
            jax.ShapeDtypeStruct((12, 4, LOCAL), F32),
        ),
        in_specs=[anywhere] * 6,
        out_specs=(anywhere, pl.BlockSpec(memory_space=pltpu.VMEM)),
        scratch_shapes=[
            inputs,
            inputs,
            pltpu.VMEM((D, 3 * LOCAL), BF16),
            pltpu.VMEM((LOCAL, D), BF16),
            wide,
            wide,
            wide,
            wide,
            pltpu.VMEM((2, PAIRS, 2, COLS, COLS), BF16),
            pltpu.VMEM((2, PAIRS, 2, 496, COLS), BF16),
            pltpu.VMEM((2, PAIRS, 2, COLS, COLS), BF16),
            pltpu.VMEM((ROWS * COLS, 4 * LOCAL), BF16),
            pltpu.VMEM((ROWS, COLS, LOCAL), BF16),
            pltpu.VMEM((2, LOCAL, 2 * LOCAL), BF16),
            pltpu.VMEM((2, 496, 2 * LOCAL), BF16),
            pltpu.VMEM((2, LOCAL + 8, 2 * LOCAL), F32),
            pltpu.VMEM((COLS, LOCAL), F32),
            dma((2, PAIRS, 26)),
            dma((2, PAIRS, 26)),
            dma((15,)),
            dma((ROWS, 4)),
            dma((ROWS, 4)),
            dma((2,)),
            dma((2,)),
            dma((2, 13)),
            dma((2, 13)),
            dma((ROWS,)),
        ],
        compiler_params=pltpu.CompilerParams(
            collective_id=0, has_side_effects=True, vmem_limit_bytes=63 * 2**20
        ),
        cost_estimate=pl.CostEstimate(
            flops=27 * 10**9, bytes_accessed=16 * 10**6, transcendentals=10**6
        ),
        name="row_attention_backward",
    )(
        tokens.reshape(-1, model_width), cotangent.reshape(-1, model_width),
        w_query, w_key, w_value, w_out,
    )

    return token_grads.reshape(leading, rows_here, columns, LOCAL), weight_grads


def solution(mesh):
    return jax.shard_map(
        local,
        mesh=mesh,
        in_specs=(
            P("aln", "row", None, None),
            P(None, "head"),
            P(None, "head"),
            P(None, "head"),
            P("head", None),
            P("aln", "row", None, None),
        ),
        out_specs=(P("aln", "row", None, "head"), P(("aln", "row"), None, "head")),
        check_vma=False,
    )
```
